32 devices in a mesh: slab: 8 (over z, x), orb: 4 (over y, core).
Axes of the slice: x: 2, y: 2, z: 4, core: 2. Of those that a mesh axis runs over, the one named last changes fastest.
Arguments:
- orbitals: bfloat16 [8, 4, 1, 64, 2304], P(None, 'orb', None, 'slab'), may hold values from -6 to 6
- potential: float32 [64, 2304], P('slab'), may hold values from -1.5 to 0.5
- partners: int32 [8, 4, 1, 2], P('slab', 'orb'), may hold values from 0 to 31, as said below
- pair_valid: int32 [8, 4, 1, 2], P('slab', 'orb'), may hold values from 0 to 1, as said below
Outputs:
- action: bfloat16 [8, 4, 1, 64, 2304], P(None, 'orb', None, 'slab')
The draws below stay inside these ranges and needn't reach their ends.
Inputs may be any that keep to these rules, and one draw needn't show every extreme that they name: partners names, for orbital number n = (a * 4 + b) + r, an orbital number that differs from n by 1 to 1 along the cyclic order of the 32 orbitals: ahead of n in even slots, behind n in odd slots; a partner may be listed more than once. `pair_valid`: slot 0 of every orbital is used.
All inputs are finite; a program needn't handle non-finite values.
Results may differ from the reference program's by a relative error of at most 0.001.
Values may be sent and summed in bfloat16 or wider, within the bound.
A program may use at most 64 MiB of HBM per device.

```python
import math
import jax
import jax.numpy as jnp
from jax import lax

NX = 48
NY = 48
NZ = 64
ORB_DEV = 1
SLOTS = 2
NYX = 2304
SLABS = 8
BLOCKS = 4
NORB = 32


def draw_partners(key, part):
    size_key = jax.random.fold_in(key, 17)
    shape = (SLABS, BLOCKS, ORB_DEV, SLOTS)
    distance = jax.random.randint(size_key, shape, 1, ORB_DEV + 1)
    slot_index = jnp.arange(SLOTS, dtype=jnp.int32).reshape(1, 1, 1, SLOTS)
    direction = 1 - 2 * (slot_index % 2)
    own_number = jnp.arange(NORB, dtype=jnp.int32).reshape(SLABS, BLOCKS, ORB_DEV, 1)
    return ((own_number + direction * distance) % NORB).astype(jnp.int32)


def draw_pair_valid(key, part):
    flag_key = jax.random.fold_in(key, 29)
    shape = (SLABS, BLOCKS, ORB_DEV, SLOTS)
    drawn = (jax.random.randint(flag_key, shape, 0, 4) < 3).astype(jnp.int32)
    slot_index = jnp.arange(SLOTS, dtype=jnp.int32).reshape(1, 1, 1, SLOTS)
    return jnp.where(slot_index == 0, 1, drawn).astype(jnp.int32)


def levels(own_key, dims, cuts, smallest, top_value):
    def one(dim, shards_of):
        steps = jax.random.uniform(jax.random.fold_in(jax.random.fold_in(own_key, 6), dim), (shards_of,), jnp.float32, smallest / len(cuts), top_value / len(cuts))
        return jnp.repeat(jnp.exp(steps), dims[dim] // shards_of).reshape((-1,) + (1,) * (len(dims) - dim - 1))

    gain = one(*cuts[0])
    for cut in cuts[1:]:
        gain = gain * one(*cut)
    return gain


def gaussian(rng, extent, deviation, limit, pieces=(), held_as=jnp.bfloat16):
    entries = jax.random.normal(rng, extent, jnp.float32) * deviation
    if len(pieces) > 0:
        entries = levels(rng, extent, pieces, -0.22, 0.18) * entries
    return jnp.clip(entries, min=-limit, max=limit).astype(held_as)


def setup_inputs(seed: int = 0) -> dict:
    arg_keys = jax.random.split(jax.random.key(seed), 5)
    return {
        "orbitals": gaussian(arg_keys[0], (SLABS, BLOCKS, ORB_DEV, NZ, NYX), 1.0, 6.0, ((1, 4), (3, 8))),
        "potential": jnp.clip(-1.5 + 2.0 * jax.random.uniform(arg_keys[1], (NZ, NYX), jnp.float32) ** levels(arg_keys[1], (NZ, NYX), ((0, 8),), -0.2, 0.2), -1.5, 0.5),
        "partners": draw_partners(jax.random.fold_in(arg_keys[4], 71), 0),
        "pair_valid": draw_pair_valid(jax.random.fold_in(arg_keys[4], 71), 0),
    }


stencil_weights = (-205.0 / 72.0, 8.0 / 5.0, -1.0 / 5.0, 8.0 / 315.0, -1.0 / 560.0)
screening = 0.11
mixing = 0.25


def squared_wave(length):
    grid = jnp.arange(length, dtype=jnp.int32)
    folded = jnp.minimum(grid, length - grid).astype(jnp.float32)
    return (2.0 * math.pi * folded / length) * (2.0 * math.pi * folded / length)


def screened_kernel(depth, rows, cols):
    wave = squared_wave(depth)[:, None, None] + squared_wave(rows)[None, :, None] + squared_wave(cols)[None, None, :]
    safe = jnp.where(wave > 0, wave, 1.0)
    inner = 4.0 * math.pi / safe * (1.0 - jnp.exp(-safe / (4.0 * screening * screening)))
    return jnp.where(wave > 0, inner, math.pi / (screening * screening))


def reference(orbitals, potential, partners, pair_valid):
    total = orbitals.shape[0] * orbitals.shape[1] * orbitals.shape[2]
    values = orbitals.astype(jnp.float32).reshape(total, NZ, NY, NX)
    laplace = 3.0 * stencil_weights[0] * values
    for reach in range(1, 5):
        for axis_index in (1, 2, 3):
            laplace = laplace + stencil_weights[reach] * (jnp.roll(values, reach, axis_index) + jnp.roll(values, -reach, axis_index))
    kernel = screened_kernel(NZ, NY, NX)
    lists = partners.reshape(total, SLOTS)
    weights = pair_valid.reshape(total, SLOTS).astype(jnp.float32)

    def turn(accum, slot):
        lister = slot // SLOTS
        column = slot % SLOTS
        partner = lists[lister, column]
        weight = weights[lister, column]
        first = values[lister]
        second = values[partner]
        field = jnp.fft.ifftn(kernel * jnp.fft.fftn(first * second)).real * weight
        accum = accum.at[lister].add(field * second)
        accum = accum.at[partner].add(field * first)
        return accum, None

    slots = jnp.arange(total * SLOTS, dtype=jnp.int32)
    exchange, unused = lax.scan(turn, jnp.zeros_like(values), slots)
    grid_potential = potential.reshape(1, NZ, NY, NX)
    result = -0.5 * laplace + grid_potential * values - mixing * exchange
    return result.reshape(orbitals.shape).astype(jnp.bfloat16)
```

```python
import functools
import math

import jax
import jax.numpy as jnp
import ml_dtypes
import numpy as np
from jax import lax
from jax.experimental import pallas as pl
from jax.experimental.pallas import tpu as pltpu
from jax.sharding import PartitionSpec as P

NX = 48
NY = 48
NZ = 64
NYX = NY * NX
LANES = 128
GROUP = 4
CHUNKS = 3

stencil_weights = (-205.0 / 72.0, 8.0 / 5.0, -1.0 / 5.0, 8.0 / 315.0, -1.0 / 560.0)
screening = 0.11
mixing = 0.25
MESH = pl.DeviceIdType.MESH


def squared_wave(length):
    grid = np.arange(length)
    folded = np.minimum(grid, length - grid).astype(np.float64)
    return (2.0 * math.pi * folded / length) ** 2


def screened_kernel():
    wave = (
        squared_wave(NX)[:, None, None]
        + squared_wave(NY)[None, :, None]
        + squared_wave(NZ)[None, None, :]
    )
    safe = np.where(wave > 0, wave, 1.0)
    inner = 4.0 * math.pi / safe * (1.0 - np.exp(-safe / (4.0 * screening * screening)))
    table = np.where(wave > 0, inner, math.pi / (screening * screening)) / (NX * NY * NZ)
    return np.concatenate([table, table], axis=2).astype(np.float32)


def split(matrix):
    high = matrix.astype(ml_dtypes.bfloat16)
    low = (matrix - high.astype(np.float64)).astype(ml_dtypes.bfloat16)
    return high, low


def hartley(length):
    grid = np.arange(length)
    angle = (grid[:, None] * grid[None, :] % length) * (2.0 * math.pi / length)
    return np.cos(angle) + np.sin(angle)


def left_table(length):
    high, low = split(hartley(length))
    return np.concatenate([high, low, high], axis=1)


def depth_table():
    high, low = split(np.kron(np.eye(2), hartley(NZ)))
    upper = np.concatenate([high, low], axis=1)
    lower = np.concatenate([high, np.zeros_like(low)], axis=1)
    return np.concatenate([upper, lower], axis=0)


def vertical_table():
    total = 3.0 * stencil_weights[0] * np.eye(NZ)
    for reach in range(1, 5):
        turned = np.roll(np.eye(NZ), reach, axis=0)
        total = total + stencil_weights[reach] * (turned + turned.T)
    high, low = split(-0.5 * total)
    return np.concatenate([high, low], axis=1)


def parts(data):
    high = data.astype(jnp.bfloat16)
    low = (data - high.astype(jnp.float32)).astype(jnp.bfloat16)
    return high, low


def from_left(table, data):
    high, low = parts(data)
    return jnp.dot(
        table, jnp.concatenate([high, high, low], axis=0), preferred_element_type=jnp.float32
    )


def from_right(data, table):
    high, low = parts(data)
    both = jnp.dot(
        jnp.concatenate([high, low], axis=1), table, preferred_element_type=jnp.float32
    )
    return both[:, :LANES] + both[:, LANES:]


def lateral(field):
    column = lax.broadcasted_iota(jnp.int32, field.shape, 1) % NX
    total = jnp.zeros_like(field)
    for reach in range(1, 5):
        along_y = pltpu.roll(field, reach * NX, 1) + pltpu.roll(field, NYX - reach * NX, 1)
        upper = jnp.where(
            column + reach < NX,
            pltpu.roll(field, NYX - reach, 1),
            pltpu.roll(field, NX - reach, 1),
        )
        lower = jnp.where(
            column >= reach,
            pltpu.roll(field, reach, 1),
            pltpu.roll(field, NYX + reach - NX, 1),
        )
        total = total + (-0.5 * stencil_weights[reach]) * (along_y + upper + lower)
    return total


def body(
    slabs, orbs, depth,
    orb_ref, pot_ref, flag_ref, side_ref, deep_ref, vert_ref, green_ref,
    out_ref,
    landed, wide, lap, vbuf, wbuf, field_a, field_b, ready,
    in_send, in_recv, fwd_send, fwd_recv, v_send, v_recv, w_send, w_recv,
    out_send, out_recv, here_sem,
):
    me = lax.axis_index("slab")
    orb = lax.axis_index("orb")
    number = me * orbs + orb
    after = lax.rem(number + 1, slabs * orbs)
    before = lax.rem(number + slabs * orbs - 1, slabs * orbs)
    right = (after // orbs, lax.rem(after, orbs))
    left = (before // orbs, lax.rem(before, orbs))

    def ahead(k):
        return lax.rem(me + k, slabs)

    def behind(k):
        return lax.rem(me + slabs - k, slabs)

    def remote(src, dst, send, recv, device):
        return pltpu.make_async_remote_copy(
            src_ref=src, dst_ref=dst, send_sem=send, recv_sem=recv,
            device_id=device, device_id_type=MESH,
        )

    barrier = pltpu.get_barrier_semaphore()
    for k in range(1, slabs):
        pl.semaphore_signal(barrier, inc=1, device_id=(ahead(k), orb), device_id_type=MESH)
    for device in (left, right):
        pl.semaphore_signal(barrier, inc=1, device_id=device, device_id_type=MESH)
    own_in = pltpu.make_async_copy(orb_ref.at[me], landed.at[1, me], here_sem.at[0])
    own_in.start()
    own_v = pltpu.make_async_copy(pot_ref, vbuf.at[me], here_sem.at[1])
    own_v.start()
    pl.semaphore_wait(barrier, slabs + 1)

    sends = []

    def start(copy):
        copy.start()
        sends.append(copy)
        return copy

    for k in range(1, slabs):
        start(remote(orb_ref.at[ahead(k)], landed.at[1, me], in_send.at[k], in_recv.at[k],
                     (ahead(k), orb)))

    def forward(k):
        source = behind(k)
        start(remote(landed.at[1, source], landed.at[0, source], fwd_send.at[0, k],
                     fwd_recv.at[0, k], right))
        start(remote(landed.at[1, source], landed.at[2, source], fwd_send.at[1, k],
                     fwd_recv.at[1, k], left))

    own_in.wait()
    forward(0)
    start(remote(flag_ref, wbuf.at[0], w_send.at[0], w_recv.at[0], right))
    start(remote(flag_ref, wbuf.at[1], w_send.at[1], w_recv.at[1], left))
    for k in range(1, slabs):
        source = behind(k)
        remote(orb_ref.at[me], landed.at[1, source], in_send.at[k], in_recv.at[k],
               (source, orb)).wait_recv()
        forward(k)
    own_v.wait()
    for k in range(1, slabs):
        start(remote(pot_ref, vbuf.at[me], v_send.at[k], v_recv.at[k], (ahead(k), orb)))

    for s in range(slabs):
        wide[1, s * depth : (s + 1) * depth, :] = landed[1, s].astype(jnp.float32)

    def lateral_turn(r, carry):
        rows = pl.ds(pl.multiple_of(r * 8, 8), 8)
        lap[rows, :] = lateral(wide[1, rows, :])
        return carry

    lax.fori_loop(0, NZ // 8, lateral_turn, 0)

    def vertical_turn(j, carry):
        lanes = pl.ds(pl.multiple_of(j * 256, 256), 256)
        values = wide[1, :, lanes].astype(jnp.bfloat16)
        lap[:, lanes] += jnp.dot(
            vert_ref[...], jnp.concatenate([values, values], axis=0),
            preferred_element_type=jnp.float32,
        )
        return carry

    lax.fori_loop(0, NYX // 256, vertical_turn, 0)

    for k in range(slabs):
        for side, sender in ((0, left), (1, right)):
            remote(landed.at[1, k], landed.at[2 * side, (sender[0] + slabs - k) % slabs],
                   fwd_send.at[side, k], fwd_recv.at[side, k], sender).wait_recv()
    for s in range(slabs):
        for side in (0, 2):
            wide[side, s * depth : (s + 1) * depth, :] = landed[side, s].astype(jnp.float32)

    def turn_in(j, carry):
        for t in range(2):
            lanes = pl.ds(pl.multiple_of((2 * j + t) * LANES, LANES), LANES)
            own = wide[1, :, lanes]
            stacked = jnp.concatenate([own * wide[2, :, lanes], own * wide[0, :, lanes]], axis=0)
            field_a[lanes, :] = stacked.T
        return carry

    lax.fori_loop(0, NYX // LANES // 2, turn_in, 0)

    def along_x(source, target):
        def turn(i, carry):
            base = i * (2 * GROUP)
            loaded = []
            for g in range(GROUP):
                halves = [
                    source[pl.ds(pl.multiple_of((base + 2 * g + t) * NX, NX), NX), :]
                    for t in range(2)
                ]
                loaded.append(jnp.concatenate(halves, axis=1))
            done = [from_left(side_ref[...], data) for data in loaded]
            for g in range(GROUP):
                for t in range(2):
                    rows = pl.ds(pl.multiple_of((base + 2 * g + t) * NX, NX), NX)
                    target[rows, :] = done[g][:, t * LANES : (t + 1) * LANES]
            return carry

        lax.fori_loop(0, NY // (2 * GROUP), turn, 0)

    def along_yz(source, target):
        def turn(i, carry):
            base = i * (2 * GROUP)
            data = []
            for g in range(GROUP):
                halves = [source[pl.ds(base + 2 * g + t, NY, stride=NX), :] for t in range(2)]
                data.append(jnp.concatenate(halves, axis=1))
            data = [from_left(side_ref[...], d) for d in data]
            data = [jnp.concatenate([d[:, :LANES], d[:, LANES:]], axis=0) for d in data]
            data = [from_right(d, deep_ref[...]) for d in data]
            greens = [
                jnp.concatenate([green_ref[base + 2 * g], green_ref[base + 2 * g + 1]], axis=0)
                for g in range(GROUP)
            ]
            data = [d * green for d, green in zip(data, greens)]
            data = [from_right(d, deep_ref[...]) for d in data]
            data = [jnp.concatenate([d[:NY], d[NY:]], axis=1) for d in data]
            data = [from_left(side_ref[...], d) for d in data]
            for g in range(GROUP):
                for t in range(2):
                    target[pl.ds(base + 2 * g + t, NY, stride=NX), :] = data[g][
                        :, t * LANES : (t + 1) * LANES
                    ]
            return carry

        lax.fori_loop(0, NX // (2 * GROUP), turn, 0)

    along_x(field_a, field_b)
    along_yz(field_b, field_a)
    along_x(field_a, field_b)

    for k in range(1, slabs):
        source = behind(k)
        remote(pot_ref, vbuf.at[source], v_send.at[k], v_recv.at[k], (source, orb)).wait_recv()
    remote(flag_ref, wbuf.at[0], w_send.at[0], w_recv.at[0], left).wait_recv()
    remote(flag_ref, wbuf.at[1], w_send.at[1], w_recv.at[1], right).wait_recv()
    weight_next = -mixing * (flag_ref[0, 0:1, :] + wbuf[1, 1, 0:1, :])
    weight_last = -mixing * (flag_ref[1, 0:1, :] + wbuf[0, 0, 0:1, :])

    span = NYX // CHUNKS

    def turn_out(j, carry):
        lanes = pl.ds(pl.multiple_of(j * LANES, LANES), LANES)
        pots = field_b[lanes, :].T
        terms = (
            lap[:, lanes]
            + weight_next * (pots[:NZ] * wide[2, :, lanes])
            + weight_last * (pots[NZ:] * wide[0, :, lanes])
        )
        own = wide[1, :, lanes]
        for s in range(slabs):
            rows = slice(s * depth, (s + 1) * depth)
            ready[s, :, lanes] = (terms[rows] + vbuf[s, :, lanes] * own[rows]).astype(jnp.bfloat16)
        return carry

    tiles = span // LANES
    for c in range(CHUNKS):
        lax.fori_loop(c * tiles, (c + 1) * tiles, turn_out, 0)
        lanes = pl.ds(c * span, span)
        for k in range(1, slabs):
            peer = ahead(k)
            start(remote(ready.at[peer, :, lanes], out_ref.at[me, :, lanes], out_send.at[c, k],
                         out_recv.at[c, k], (peer, orb)))
    own_out = pltpu.make_async_copy(ready.at[me], out_ref.at[me], here_sem.at[0])
    own_out.start()
    for c in range(CHUNKS):
        lanes = pl.ds(c * span, span)
        for k in range(1, slabs):
            source = behind(k)
            remote(ready.at[me, :, lanes], out_ref.at[source, :, lanes], out_send.at[c, k],
                   out_recv.at[c, k], (source, orb)).wait_recv()
    for copy in sends:
        copy.wait_send()
    own_out.wait()


def local(orbitals, potential, partners, pair_valid):
    slabs, depth = orbitals.shape[0], orbitals.shape[3]
    orbs = lax.axis_size("orb")
    flags = jnp.broadcast_to(
        pair_valid.reshape(2, 1, 1).astype(jnp.float32), (2, 8, LANES)
    )
    dma = pltpu.SemaphoreType.DMA
    any_space = pl.BlockSpec(memory_space=pl.ANY)
    vmem = pl.BlockSpec(memory_space=pltpu.VMEM)
    result = pl.pallas_call(
        functools.partial(body, slabs, orbs, depth),
        out_shape=jax.ShapeDtypeStruct((slabs, depth, NYX), jnp.bfloat16),
        in_specs=[any_space, any_space, vmem, vmem, vmem, vmem, vmem],
        out_specs=any_space,
        scratch_shapes=[
            pltpu.VMEM((3, slabs, depth, NYX), jnp.bfloat16),
            pltpu.VMEM((3, NZ, NYX), jnp.float32),
            pltpu.VMEM((NZ, NYX), jnp.float32),
            pltpu.VMEM((slabs, depth, NYX), jnp.float32),
            pltpu.VMEM((2, 2, 8, LANES), jnp.float32),
            pltpu.VMEM((NYX, LANES), jnp.float32),
            pltpu.VMEM((NYX, LANES), jnp.float32),
            pltpu.VMEM((slabs, depth, NYX), jnp.bfloat16),
            dma((slabs,)), dma((slabs,)),
            dma((2, slabs)), dma((2, slabs)),
            dma((slabs,)), dma((slabs,)),
            dma((2,)), dma((2,)),
            dma((CHUNKS, slabs)), dma((CHUNKS, slabs)),
            dma((2,)),
        ],
        compiler_params=pltpu.CompilerParams(
            collective_id=0, has_side_effects=True, vmem_limit_bytes=40 * 1024 * 1024
        ),
        cost_estimate=pl.CostEstimate(
            flops=2 * 1024 * 1024 * 1024, bytes_accessed=8 * 1024 * 1024, transcendentals=0
        ),
    )(
        orbitals.reshape(slabs, depth, NYX), potential, flags,
        jnp.asarray(left_table(NX)), jnp.asarray(depth_table()), jnp.asarray(vertical_table()),
        jnp.asarray(screened_kernel()),
    )
    return result.reshape(orbitals.shape)


def solution(mesh):
    in_specs = (
        P(None, "orb", None, "slab", None),
        P("slab", None),
        P("slab", "orb", None, None),
        P("slab", "orb", None, None),
    )
    out_specs = P(None, "orb", None, "slab", None)
    return jax.shard_map(local, mesh=mesh, in_specs=in_specs, out_specs=out_specs, check_vma=False)
```

```python
import functools
import math

import jax
import jax.numpy as jnp
import ml_dtypes
import numpy as np
from jax import lax
from jax.experimental import pallas as pl
from jax.experimental.pallas import tpu as pltpu
from jax.sharding import PartitionSpec as P

NX = 48
NY = 48
NZ = 64
NYX = NY * NX
LANES = 128
GROUP = 4
CHUNKS = 3

stencil_weights = (-205.0 / 72.0, 8.0 / 5.0, -1.0 / 5.0, 8.0 / 315.0, -1.0 / 560.0)
screening = 0.11
mixing = 0.25
MESH = pl.DeviceIdType.MESH


def squared_wave(length):
    grid = np.arange(length)
    folded = np.minimum(grid, length - grid).astype(np.float64)
    return (2.0 * math.pi * folded / length) ** 2


def screened_kernel():
    wave = (
        squared_wave(NX)[:, None, None]
        + squared_wave(NY)[None, :, None]
        + squared_wave(NZ)[None, None, :]
    )
    safe = np.where(wave > 0, wave, 1.0)
    inner = 4.0 * math.pi / safe * (1.0 - np.exp(-safe / (4.0 * screening * screening)))
    table = np.where(wave > 0, inner, math.pi / (screening * screening)) / (NX * NY * NZ)
    return np.concatenate([table, table], axis=2).astype(np.float32)


def split(matrix):
    high = matrix.astype(ml_dtypes.bfloat16)
    low = (matrix - high.astype(np.float64)).astype(ml_dtypes.bfloat16)
    return high, low


def hartley(length):
    grid = np.arange(length)
    angle = (grid[:, None] * grid[None, :] % length) * (2.0 * math.pi / length)
    return np.cos(angle) + np.sin(angle)


def left_table(length):
    high, low = split(hartley(length))
    return np.concatenate([high, low, high], axis=1)


def depth_table():
    high, low = split(np.kron(np.eye(2), hartley(NZ)))
    upper = np.concatenate([high, low], axis=1)
    lower = np.concatenate([high, np.zeros_like(low)], axis=1)
    return np.concatenate([upper, lower], axis=0)


def vertical_table():
    total = 3.0 * stencil_weights[0] * np.eye(NZ)
    for reach in range(1, 5):
        turned = np.roll(np.eye(NZ), reach, axis=0)
        total = total + stencil_weights[reach] * (turned + turned.T)
    high, low = split(-0.5 * total)
    return np.concatenate([high, low], axis=1)


def parts(data):
    high = data.astype(jnp.bfloat16)
    low = (data - high.astype(jnp.float32)).astype(jnp.bfloat16)
    return high, low


def from_left(table, data):
    high, low = parts(data)
    return jnp.dot(
        table, jnp.concatenate([high, high, low], axis=0), preferred_element_type=jnp.float32
    )


def from_right(data, table):
    high, low = parts(data)
    both = jnp.dot(
        jnp.concatenate([high, low], axis=1), table, preferred_element_type=jnp.float32
    )
    return both[:, :LANES] + both[:, LANES:]


def lateral(field):
    column = lax.broadcasted_iota(jnp.int32, field.shape, 1) % NX
    total = jnp.zeros_like(field)
    for reach in range(1, 5):
        along_y = pltpu.roll(field, reach * NX, 1) + pltpu.roll(field, NYX - reach * NX, 1)
        upper = jnp.where(
            column + reach < NX,
            pltpu.roll(field, NYX - reach, 1),
            pltpu.roll(field, NX - reach, 1),
        )
        lower = jnp.where(
            column >= reach,
            pltpu.roll(field, reach, 1),
            pltpu.roll(field, NYX + reach - NX, 1),
        )
        total = total + (-0.5 * stencil_weights[reach]) * (along_y + upper + lower)
    return total


def body(
    slabs, orbs, depth,
    orb_ref, pot_ref, valid_ref, side_hbm, deep_hbm, vert_hbm, green_hbm,
    out_ref,
    landed, wide, lap, vbuf, wbuf, field_a, field_b, ready,
    flag_ref, side_ref, deep_ref, vert_ref, green_ref,
    in_send, in_recv, fwd_send, fwd_recv, v_send, v_recv, w_send, w_recv,
    out_send, out_recv, here_sem,
):
    me = lax.axis_index("slab")
    orb = lax.axis_index("orb")
    number = me * orbs + orb
    after = lax.rem(number + 1, slabs * orbs)
    before = lax.rem(number + slabs * orbs - 1, slabs * orbs)
    right = (after // orbs, lax.rem(after, orbs))
    left = (before // orbs, lax.rem(before, orbs))

    def ahead(k):
        return lax.rem(me + k, slabs)

    def behind(k):
        return lax.rem(me + slabs - k, slabs)

    def remote(src, dst, send, recv, device):
        return pltpu.make_async_remote_copy(
            src_ref=src, dst_ref=dst, send_sem=send, recv_sem=recv,
            device_id=device, device_id_type=MESH,
        )

    barrier = pltpu.get_barrier_semaphore()
    for k in range(1, slabs):
        pl.semaphore_signal(barrier, inc=1, device_id=(ahead(k), orb), device_id_type=MESH)
    for device in (left, right):
        pl.semaphore_signal(barrier, inc=1, device_id=device, device_id_type=MESH)
    half = NYX // 2
    mine = pl.ds(pl.multiple_of(lax.rem(orb, 2) * half, LANES), half)
    other = pl.ds(pl.multiple_of((1 - lax.rem(orb, 2)) * half, LANES), half)
    sibling = (me, orb + 1 - 2 * lax.rem(orb, 2))
    own_in = pltpu.make_async_copy(orb_ref.at[me], landed.at[1, me], here_sem.at[0])
    own_in.start()
    own_v = pltpu.make_async_copy(pot_ref.at[:, mine], vbuf.at[me, :, mine], here_sem.at[1])
    own_v.start()
    tables = [
        pltpu.make_async_copy(source, target, here_sem.at[2 + t])
        for t, (source, target) in enumerate(
            ((vert_hbm, vert_ref), (side_hbm, side_ref), (deep_hbm, deep_ref), (green_hbm, green_ref))
        )
    ]
    for table in tables:
        table.start()
    for slot in range(2):
        flag = jnp.full((8, LANES), valid_ref[0, 0, 0, slot], jnp.int32)
        flag_ref[slot] = flag.astype(jnp.float32)
    pl.semaphore_wait(barrier, slabs + 1)

    sends = []

    def start(copy):
        copy.start()
        sends.append(copy)
        return copy

    span = NYX // CHUNKS
    tiles = span // LANES
    rows_each = span // NX

    def part(c):
        return pl.ds(c * span, span)

    for c in range(CHUNKS):
        for k in range(1, slabs):
            start(remote(orb_ref.at[ahead(k), :, part(c)], landed.at[1, me, :, part(c)],
                         in_send.at[c, k], in_recv.at[c, k], (ahead(k), orb)))
    start(remote(flag_ref, wbuf.at[0], w_send.at[0], w_recv.at[0], right))
    start(remote(flag_ref, wbuf.at[1], w_send.at[1], w_recv.at[1], left))
    own_in.wait()

    def unpack(side, c):
        for s in range(slabs):
            wide[side, s * depth : (s + 1) * depth, c * span : (c + 1) * span] = landed[
                side, s, :, c * span : (c + 1) * span
            ].astype(jnp.float32)

    def vertical_turn(j, carry):
        lanes = pl.ds(pl.multiple_of(j * 256, 256), 256)
        values = wide[1, :, lanes].astype(jnp.bfloat16)
        lap[:, lanes] = jnp.dot(
            vert_ref[...], jnp.concatenate([values, values], axis=0),
            preferred_element_type=jnp.float32,
        )
        return carry

    tables[0].wait()
    for c in range(CHUNKS):
        for k in range(1, slabs):
            source = behind(k)
            remote(orb_ref.at[me, :, part(c)], landed.at[1, source, :, part(c)],
                   in_send.at[c, k], in_recv.at[c, k], (source, orb)).wait_recv()
        start(remote(landed.at[1, :, :, part(c)], landed.at[0, :, :, part(c)],
                     fwd_send.at[0, c], fwd_recv.at[0, c], right))
        start(remote(landed.at[1, :, :, part(c)], landed.at[2, :, :, part(c)],
                     fwd_send.at[1, c], fwd_recv.at[1, c], left))
        if c == CHUNKS - 1:
            own_v.wait()
            for k in range(1, slabs):
                start(remote(pot_ref.at[:, mine], vbuf.at[me, :, mine], v_send.at[k],
                             v_recv.at[k], (ahead(k), orb)))
        unpack(1, c)
        lax.fori_loop(c * span // 256, (c + 1) * span // 256, vertical_turn, 0)

    def lateral_turn(r, carry):
        rows = pl.ds(pl.multiple_of(r * 8, 8), 8)
        lap[rows, :] += lateral(wide[1, rows, :])
        return carry

    def turn_in(j, carry):
        for t in range(2):
            lanes = pl.ds(pl.multiple_of((2 * j + t) * LANES, LANES), LANES)
            own = wide[1, :, lanes]
            stacked = jnp.concatenate([own * wide[2, :, lanes], own * wide[0, :, lanes]], axis=0)
            field_a[lanes, :] = stacked.T
        return carry

    def along_x(source, target, c):
        def turn(i, carry):
            base = i * (2 * GROUP)
            loaded = []
            for g in range(GROUP):
                halves = [
                    source[pl.ds(pl.multiple_of((base + 2 * g + t) * NX, NX), NX), :]
                    for t in range(2)
                ]
                loaded.append(jnp.concatenate(halves, axis=1))
            done = [from_left(side_ref[...], data) for data in loaded]
            for g in range(GROUP):
                for t in range(2):
                    rows = pl.ds(pl.multiple_of((base + 2 * g + t) * NX, NX), NX)
                    target[rows, :] = done[g][:, t * LANES : (t + 1) * LANES]
            return carry

        each = rows_each // (2 * GROUP)
        lax.fori_loop(c * each, (c + 1) * each, turn, 0)

    tables[1].wait()
    for c in range(CHUNKS):
        if c == CHUNKS - 1:
            lax.fori_loop(0, NZ // 8, lateral_turn, 0)
        for side, sender in ((0, left), (1, right)):
            remote(landed.at[1, :, :, part(c)], landed.at[2 * side, :, :, part(c)],
                   fwd_send.at[side, c], fwd_recv.at[side, c], sender).wait_recv()
            unpack(2 * side, c)
        lax.fori_loop(c * tiles // 2, (c + 1) * tiles // 2, turn_in, 0)
        along_x(field_a, field_b, c)

    def along_yz(source, target):
        def turn(i, carry):
            base = i * (2 * GROUP)
            data = []
            for g in range(GROUP):
                halves = [source[pl.ds(base + 2 * g + t, NY, stride=NX), :] for t in range(2)]
                data.append(jnp.concatenate(halves, axis=1))
            data = [from_left(side_ref[...], d) for d in data]
            data = [jnp.concatenate([d[:, :LANES], d[:, LANES:]], axis=0) for d in data]
            data = [from_right(d, deep_ref[...]) for d in data]
            greens = [
                jnp.concatenate([green_ref[base + 2 * g], green_ref[base + 2 * g + 1]], axis=0)
                for g in range(GROUP)
            ]
            data = [d * green for d, green in zip(data, greens)]
            data = [from_right(d, deep_ref[...]) for d in data]
            data = [jnp.concatenate([d[:NY], d[NY:]], axis=1) for d in data]
            data = [from_left(side_ref[...], d) for d in data]
            for g in range(GROUP):
                for t in range(2):
                    target[pl.ds(base + 2 * g + t, NY, stride=NX), :] = data[g][
                        :, t * LANES : (t + 1) * LANES
                    ]
            return carry

        lax.fori_loop(0, NX // (2 * GROUP), turn, 0)

    tables[2].wait()
    tables[3].wait()
    along_yz(field_b, field_a)

    for k in range(1, slabs):
        source = behind(k)
        remote(pot_ref.at[:, mine], vbuf.at[source, :, mine], v_send.at[k], v_recv.at[k],
               (source, orb)).wait_recv()
    start(remote(vbuf.at[:, :, mine], vbuf.at[:, :, mine], v_send.at[0], v_recv.at[0], sibling))
    remote(flag_ref, wbuf.at[0], w_send.at[0], w_recv.at[0], left).wait_recv()
    remote(flag_ref, wbuf.at[1], w_send.at[1], w_recv.at[1], right).wait_recv()
    weight_next = -mixing * (flag_ref[0, 0:1, :] + wbuf[1, 1, 0:1, :])
    weight_last = -mixing * (flag_ref[1, 0:1, :] + wbuf[0, 0, 0:1, :])

    def turn_out(j, carry):
        lanes = pl.ds(pl.multiple_of(j * LANES, LANES), LANES)
        pots = field_b[lanes, :].T
        terms = (
            lap[:, lanes]
            + weight_next * (pots[:NZ] * wide[2, :, lanes])
            + weight_last * (pots[NZ:] * wide[0, :, lanes])
        )
        own = wide[1, :, lanes]
        for s in range(slabs):
            rows = slice(s * depth, (s + 1) * depth)
            ready[s, :, lanes] = (terms[rows] + vbuf[s, :, lanes] * own[rows]).astype(jnp.bfloat16)
        return carry

    for c in range(CHUNKS):
        along_x(field_a, field_b, c)
        if c == 0:
            remote(vbuf.at[:, :, mine], vbuf.at[:, :, other], v_send.at[0], v_recv.at[0],
                   sibling).wait_recv()
        lax.fori_loop(c * tiles, (c + 1) * tiles, turn_out, 0)
        lanes = pl.ds(c * span, span)
        for k in range(1, slabs):
            peer = ahead(k)
            start(remote(ready.at[peer, :, lanes], out_ref.at[me, :, lanes], out_send.at[c, k],
                         out_recv.at[c, k], (peer, orb)))
    own_out = pltpu.make_async_copy(ready.at[me], out_ref.at[me], here_sem.at[0])
    own_out.start()
    for c in range(CHUNKS):
        lanes = pl.ds(c * span, span)
        for k in range(1, slabs):
            source = behind(k)
            remote(ready.at[me, :, lanes], out_ref.at[source, :, lanes], out_send.at[c, k],
                   out_recv.at[c, k], (source, orb)).wait_recv()
    for copy in sends:
        copy.wait_send()
    own_out.wait()


def local(orbitals, potential, partners, pair_valid):
    slabs, depth = orbitals.shape[0], orbitals.shape[3]
    orbs = lax.axis_size("orb")
    dma = pltpu.SemaphoreType.DMA
    any_space = pl.BlockSpec(memory_space=pl.ANY)
    result = pl.pallas_call(
        functools.partial(body, slabs, orbs, depth),
        out_shape=jax.ShapeDtypeStruct((slabs, depth, NYX), jnp.bfloat16),
        in_specs=[any_space, any_space, pl.BlockSpec(memory_space=pltpu.SMEM)] + [any_space] * 4,
        out_specs=any_space,
        scratch_shapes=[
            pltpu.VMEM((3, slabs, depth, NYX), jnp.bfloat16),
            pltpu.VMEM((3, NZ, NYX), jnp.float32),
            pltpu.VMEM((NZ, NYX), jnp.float32),
            pltpu.VMEM((slabs, depth, NYX), jnp.float32),
            pltpu.VMEM((2, 2, 8, LANES), jnp.float32),
            pltpu.VMEM((NYX, LANES), jnp.float32),
            pltpu.VMEM((NYX, LANES), jnp.float32),
            pltpu.VMEM((slabs, depth, NYX), jnp.bfloat16),
            pltpu.VMEM((2, 8, LANES), jnp.float32),
            pltpu.VMEM((NX, 3 * NX), jnp.bfloat16),
            pltpu.VMEM((4 * NZ, 4 * NZ), jnp.bfloat16),
            pltpu.VMEM((NZ, 2 * NZ), jnp.bfloat16),
            pltpu.VMEM((NX, NY, LANES), jnp.float32),
            dma((CHUNKS, slabs)), dma((CHUNKS, slabs)),
            dma((2, CHUNKS)), dma((2, CHUNKS)),
            dma((slabs,)), dma((slabs,)),
            dma((2,)), dma((2,)),
            dma((CHUNKS, slabs)), dma((CHUNKS, slabs)),
            dma((6,)),
        ],
        compiler_params=pltpu.CompilerParams(
            collective_id=0, has_side_effects=True, vmem_limit_bytes=60 * 1024 * 1024
        ),
        cost_estimate=pl.CostEstimate(
            flops=2 * 1024 * 1024 * 1024, bytes_accessed=8 * 1024 * 1024, transcendentals=0
        ),
    )(
        orbitals.reshape(slabs, depth, NYX), potential, pair_valid,
        jnp.asarray(left_table(NX)), jnp.asarray(depth_table()), jnp.asarray(vertical_table()),
        jnp.asarray(screened_kernel()),
    )
    return result.reshape(orbitals.shape)


def solution(mesh):
    in_specs = (
        P(None, "orb", None, "slab", None),
        P("slab", None),
        P("slab", "orb", None, None),
        P("slab", "orb", None, None),
    )
    out_specs = P(None, "orb", None, "slab", None)
    return jax.shard_map(local, mesh=mesh, in_specs=in_specs, out_specs=out_specs, check_vma=False)
```
